32 devices in a mesh: parts: 2 (over x), gx: 8 (over z, y), gz: 2 (over core).
Axes of the slice: x: 2, y: 2, z: 4, core: 2. Of those that a mesh axis runs over, the one named last changes fastest.
Arguments:
- velocity: float32 [3, 128, 256, 256], P(None, 'gx', 'parts', 'gz'), parts along dimension 2, may hold values from -3 to 3
- turbulence: float32 [128, 256, 256], P('gx', 'parts', 'gz'), parts along dimension 1, may hold values from 0.05 to 1
- wall_distance: float32 [128, 256, 256], P('gx', 'parts', 'gz'), parts along dimension 1, may hold values from 0.5 to 4
- porosity: float32 [128, 256, 256], P('gx', 'parts', 'gz'), parts along dimension 1, may hold values from 0.1 to 2
- solid_mask: int32 [128, 256, 256], P('gx', 'parts', 'gz'), parts along dimension 1, may hold values 0 or 1
- adj_velocity: float32 [3, 128, 256, 256], P(None, 'gx', 'parts', 'gz'), parts along dimension 2, may hold values from -6 to 6
- adj_pressure: float32 [128, 256, 256], P('gx', 'parts', 'gz'), parts along dimension 1, may hold values from -6 to 6
- adj_turbulence: float32 [128, 256, 256], P('gx', 'parts', 'gz'), parts along dimension 1, may hold values from -6 to 6
- adj_distance: float32 [128, 256, 256], P('gx', 'parts', 'gz'), parts along dimension 1, may hold values from -6 to 6
Outputs:
- new_velocity: float32 [3, 128, 256, 256], P(None, 'gx', 'parts', 'gz'), parts along dimension 2
- new_pressure: float32 [128, 256, 256], P('gx', 'parts', 'gz'), parts along dimension 1
- new_turbulence: float32 [128, 256, 256], P('gx', 'parts', 'gz'), parts along dimension 1
- new_distance: float32 [128, 256, 256], P('gx', 'parts', 'gz'), parts along dimension 1
- sensitivity: float32 [128, 256, 256], P('gx', 'parts', 'gz'), parts along dimension 1
- norms: float32 [16], P('parts'), parts along dimension 0
The draws below stay inside these ranges and needn't reach their ends.
There are 2 independent parts, one for each index of `parts`. The reference program is written for one: setup_inputs(seed, part) draws one part's arguments, and reference() takes and returns one part's arrays. A program takes and returns all parts, laid end to end along the dimension named above; each array names one. Nothing has to cross between parts.
Inputs may be any that keep to these rules, and one draw needn't show every extreme that they name: `solid_mask`: 1 marks a solid cell, 0 a fluid cell.
All inputs are finite; a program needn't handle non-finite values. No bound on the sum of `solid_mask` on one device may be relied on, other than what follows from the above.
Results may differ from the reference program's by a relative error of at most 0.0001.
Values sent between devices are 32-bit elements; how exact they have to be, the bound alone decides.
A program may use at most 128 MiB of HBM per device.

```python
import math
import jax
import jax.numpy as jnp
from jax import lax

SWEEPS = 2
NX = 128
NY = 128
NZ = 256


def place_ends(result, key, least, top_value):
    spot = [jax.random.randint(jax.random.fold_in(key, axis), (), 0, length) for axis, length in enumerate(result.shape)]
    widest = result.shape.index(max(result.shape))
    neighbour = spot[:widest] + [(spot[widest] + 1) % result.shape[widest]] + spot[widest + 1:]
    return result.at[tuple(spot)].set(least).at[tuple(neighbour)].set(top_value)


def shard_levels(own_key, dims, split, least, largest):
    def one(axis_at, parts):
        steps = jax.random.uniform(jax.random.fold_in(jax.random.fold_in(own_key, 6), axis_at), (parts,), jnp.float32, least / len(split), largest / len(split))
        return jnp.repeat(jnp.exp(steps), dims[axis_at] // parts).reshape((-1,) + (1,) * (len(dims) - axis_at - 1))

    gain = one(*split[0])
    for cut in split[1:]:
        gain = gain * one(*cut)
    return gain


def noise(own_key, shape, width, bound, cuts=(), dtype=jnp.bfloat16):
    gain = shard_levels(own_key, shape, cuts, -0.22, 0.18) if cuts else 1.0
    drawn = jax.random.normal(own_key, shape, jnp.float32) * width * gain
    return jnp.minimum(jnp.maximum(drawn, -bound), bound).astype(dtype)


def setup_inputs(seed: int = 0, part: int = 0) -> dict:
    streams_of = jax.random.split(jax.random.key(seed), 10)
    part_splits = jax.random.split(jax.random.fold_in(streams_of[9], part), 10)
    velocity = noise(part_splits[0], (3, NX, NY, NZ), 0.5, 3.0, ((1, 8), (3, 2)), jnp.float32)
    turbulence = jnp.clip(jnp.exp(math.log(1.0) - 2.9957323 * jax.random.uniform(part_splits[1], (NX, NY, NZ), jnp.float32) ** shard_levels(part_splits[1], (NX, NY, NZ), ((0, 8), (2, 2)), -0.2, 0.2)), 0.05, 1.0)
    wall_distance = jnp.clip(jnp.exp(math.log(4.0) - 2.0794415 * jax.random.uniform(part_splits[2], (NX, NY, NZ), jnp.float32) ** shard_levels(part_splits[2], (NX, NY, NZ), ((0, 8), (2, 2)), -0.2, 0.2)), 0.5, 4.0)
    porosity = jnp.clip(jnp.exp(math.log(2.0) - 2.9957323 * jax.random.uniform(part_splits[3], (NX, NY, NZ), jnp.float32) ** shard_levels(part_splits[3], (NX, NY, NZ), ((0, 8), (2, 2)), -0.2, 0.2)), 0.1, 2.0)
    solid_mask = place_ends((jax.random.randint(part_splits[4], (NX, NY, NZ), 0, 8) < 1).astype(jnp.int32), jax.random.fold_in(part_splits[4], 1), 0, 1)
    adj_velocity = noise(part_splits[5], (3, NX, NY, NZ), 1.0, 6.0, ((1, 8), (3, 2)), jnp.float32)
    adj_pressure = noise(part_splits[6], (NX, NY, NZ), 1.0, 6.0, ((0, 8), (2, 2)), jnp.float32)
    adj_turbulence = noise(part_splits[7], (NX, NY, NZ), 1.0, 6.0, ((0, 8), (2, 2)), jnp.float32)
    adj_distance = noise(part_splits[8], (NX, NY, NZ), 1.0, 6.0, ((0, 8), (2, 2)), jnp.float32)
    return dict(velocity=velocity, turbulence=turbulence, wall_distance=wall_distance, porosity=porosity, solid_mask=solid_mask, adj_velocity=adj_velocity, adj_pressure=adj_pressure, adj_turbulence=adj_turbulence, adj_distance=adj_distance)


VISCOSITY = 0.5
COUPLING = 0.6
DESTRUCTION = 0.3
DISTANCE_DAMPING = 0.5
PENALTY = 20.0

def stencil(field):
    centre = field[:, 1:-1, 1:-1, 1:-1]
    x_plus = field[:, 2:, 1:-1, 1:-1]
    x_minus = field[:, :-2, 1:-1, 1:-1]
    y_plus = field[:, 1:-1, 2:, 1:-1]
    y_minus = field[:, 1:-1, :-2, 1:-1]
    z_plus = field[:, 1:-1, 1:-1, 2:]
    z_minus = field[:, 1:-1, 1:-1, :-2]
    laplace = x_plus + x_minus + y_plus + y_minus + z_plus + z_minus
    return (centre, laplace, 0.5 * (x_plus - x_minus), 0.5 * (y_plus - y_minus), 0.5 * (z_plus - z_minus))

def shear_square(padded_velocity):
    centre, laplace, grad_x, grad_y, grad_z = stencil(padded_velocity)
    return lax.optimization_barrier(jnp.sum(grad_x * grad_x + grad_y * grad_y + grad_z * grad_z, axis=0)) / 9.0

def coefficients(primal, shear):
    flow = primal[0:3]
    turb = primal[3]
    poros = primal[4]
    wall = primal[5]
    solid = primal[6]
    viscous = VISCOSITY + turb
    diag_flow = 6.0 * viscous + poros + PENALTY * solid
    diag_turb = 6.0 * viscous + DESTRUCTION * turb / (wall * wall)
    coupled = 2.0 * DESTRUCTION * turb * turb / (wall * wall * wall)
    return (flow, poros, viscous, diag_flow, diag_turb, shear, coupled)

def sweep(padded, coefs):
    flow, poros, viscous, diag_flow, diag_turb, shear, coupled = coefs
    previous, laplace, grad_x, grad_y, grad_z = stencil(padded)
    advect = flow[0] * grad_x + flow[1] * grad_y + flow[2] * grad_z
    adj_flow = previous[0:3]
    adj_turb = previous[4]
    press_grad = jnp.stack([grad_x[3], grad_y[3], grad_z[3]])
    flow_next = (poros * flow + viscous * laplace[0:3] + advect[0:3] - press_grad + COUPLING * flow * adj_turb) / diag_flow
    divergence = grad_x[0] + grad_y[1] + grad_z[2]
    press_next = (laplace[3] - divergence) / 6.0
    turb_next = (COUPLING * shear + COUPLING * lax.optimization_barrier(jnp.sum(flow * adj_flow, axis=0)) + viscous * laplace[4] + advect[4]) / diag_turb
    wall_next = (laplace[5] + coupled * adj_turb) / (6.0 + DISTANCE_DAMPING)
    return jnp.concatenate([flow_next, press_next[None], turb_next[None], wall_next[None]], axis=0)

def changes(updated, previous):
    delta = (updated - previous) ** 2
    return jnp.stack([jnp.sum(delta[0:3]), jnp.sum(delta[3]), jnp.sum(delta[4]), jnp.sum(delta[5])])

def pad_all(field):
    return jnp.pad(field, ((0, 0), (1, 1), (1, 1), (1, 1)))

def reference(velocity, turbulence, wall_distance, porosity, solid_mask, adj_velocity, adj_pressure, adj_turbulence, adj_distance):
    solid = solid_mask.astype(jnp.float32)
    primal = jnp.concatenate([velocity, jnp.stack([turbulence, porosity, wall_distance, solid])], axis=0)
    coefs = coefficients(primal, shear_square(pad_all(velocity)))
    adjoint = jnp.concatenate([adj_velocity, adj_pressure[None], adj_turbulence[None], adj_distance[None]], axis=0)
    totals = []
    for sweep_index in range(SWEEPS):
        updated = sweep(pad_all(adjoint), coefs)
        totals.append(changes(updated, adjoint))
        adjoint = updated
    norms = jnp.sqrt(jnp.concatenate(totals) + 1e-06)
    sensitivity = (1.0 - solid) * lax.optimization_barrier(jnp.sum(velocity * adjoint[0:3], axis=0))
    return (adjoint[0:3], adjoint[3], adjoint[4], adjoint[5], sensitivity, norms)
```

```python
import functools

import jax
import jax.numpy as jnp
from jax import lax
from jax.experimental import pallas as pl
from jax.experimental.pallas import tpu as pltpu
from jax.sharding import PartitionSpec as P

VISCOSITY = 0.5
COUPLING = 0.6
DESTRUCTION = 0.3
DISTANCE_DAMPING = 0.5
PENALTY = 20.0
PAD = 8
ROWS = 8
MESH = pl.DeviceIdType.MESH


def kernel(
    ngx,
    ngz,
    velocity,
    turbulence,
    wall_distance,
    porosity,
    solid_mask,
    adj_velocity,
    adj_pressure,
    adj_turbulence,
    adj_distance,
    new_velocity,
    new_pressure,
    new_turbulence,
    new_distance,
    sensitivity,
    norms,
    first,
    second,
    flow,
    turb,
    wall,
    poros,
    solid,
    coefs,
    edge_send,
    edge_recv,
    sums,
    all_sums,
    load_sem,
    face_send_sem,
    face_recv_sem,
    edge_send_sem,
    edge_recv_sem,
    sum_send_sem,
    sum_recv_sem,
):
    nx, ny, nz = turbulence.shape
    gx = lax.axis_index("gx")
    gz = lax.axis_index("gz")
    me = gx * ngz + gz
    group = ngx * ngz
    has_low = gx > 0
    has_high = gx < ngx - 1
    body = pl.ds(PAD, ny)
    chunks = ny // ROWS

    loads = [
        pltpu.make_async_copy(adj_velocity, first.at[0:3, 1 : nx + 1, body], load_sem.at[0]),
        pltpu.make_async_copy(adj_pressure, first.at[3, 1 : nx + 1, body], load_sem.at[1]),
        pltpu.make_async_copy(adj_turbulence, first.at[4, 1 : nx + 1, body], load_sem.at[2]),
        pltpu.make_async_copy(adj_distance, first.at[5, 1 : nx + 1, body], load_sem.at[3]),
        pltpu.make_async_copy(velocity, flow.at[:, 1 : nx + 1, body], load_sem.at[4]),
        pltpu.make_async_copy(turbulence, turb, load_sem.at[5]),
        pltpu.make_async_copy(wall_distance, wall, load_sem.at[6]),
        pltpu.make_async_copy(porosity, poros, load_sem.at[7]),
        pltpu.make_async_copy(solid_mask, solid, load_sem.at[8]),
    ]
    for load in loads:
        load.start()

    barrier = pltpu.get_barrier_semaphore()
    others = []
    for k in range(1, group):
        flat = lax.rem(me + k, group)
        others.append({"gx": lax.div(flat, ngz), "gz": lax.rem(flat, ngz)})
    for other in others:
        pl.semaphore_signal(barrier, inc=1, device_id=other, device_id_type=MESH)
    pl.semaphore_wait(barrier, group - 1)

    def face(side, slot, source, target):
        step = -1 if side == 0 else 1
        return pltpu.make_async_remote_copy(
            src_ref=source,
            dst_ref=target,
            send_sem=face_send_sem.at[side, slot],
            recv_sem=face_recv_sem.at[side, slot],
            device_id={"gx": jnp.clip(gx + step, 0, ngx - 1)},
            device_id_type=MESH,
        )

    def faces_of(side):
        plane, halo = (0, nx + 1) if side == 0 else (nx - 1, 0)
        return [
            face(side, 0, adj_velocity.at[:, plane], first.at[0:3, halo, body]),
            face(side, 1, adj_pressure.at[plane], first.at[3, halo, body]),
            face(side, 2, adj_turbulence.at[plane], first.at[4, halo, body]),
            face(side, 3, adj_distance.at[plane], first.at[5, halo, body]),
            face(side, 4, velocity.at[:, plane], flow.at[:, halo, body]),
        ]

    def later_faces_of(side):
        plane, halo = (1, nx + 1) if side == 0 else (nx, 0)
        return [face(side, 5, second.at[:, plane, body], second.at[:, halo, body])]

    sends_to = (has_low, has_high)
    takes_from = (has_high, has_low)

    def start_faces(make):
        for side in (0, 1):
            @pl.when(sends_to[side])
            def _():
                for copy in make(side):
                    copy.start()

    def wait_faces(make):
        for side in (0, 1):
            @pl.when(takes_from[side])
            def _():
                for copy in make(side):
                    copy.wait_recv()

    def finish_faces(make):
        for side in (0, 1):
            @pl.when(sends_to[side])
            def _():
                for copy in make(side):
                    copy.wait_send()

    start_faces(faces_of)

    def clear(x, carry):
        blank = jnp.zeros((PAD, nz), jnp.float32)
        for f in range(6):
            for field in (first, second):
                field[f, x, 0:PAD] = blank
                field[f, x, PAD + ny : 2 * PAD + ny] = blank
        for f in range(3):
            flow[f, x, 0:PAD] = blank
            flow[f, x, PAD + ny : 2 * PAD + ny] = blank
        return carry

    lax.fori_loop(1, nx + 1, clear, 0)
    for missing, halo in ((gx == 0, 0), (gx == ngx - 1, nx + 1)):
        @pl.when(missing)
        def _():
            blank = jnp.zeros((ny, nz), jnp.float32)
            for f in range(6):
                first[f, halo, body] = blank
                second[f, halo, body] = blank
            for f in range(3):
                flow[f, halo, body] = blank

    lane = lax.broadcasted_iota(jnp.int32, (ROWS, nz), 1)
    edge = jnp.where(gz == 0, nz - 1, 0)
    at_edge = lane == edge
    at_first = lane == 0
    at_last = lane == nz - 1

    def pack(field, count, slot):
        def step(k, carry):
            r = pl.multiple_of(k * ROWS, ROWS)
            packed = jnp.zeros((ROWS, nz), jnp.float32)
            for f in range(count):
                for x in range(nx):
                    spot = f * nx + x
                    cells = field[f, x + 1, pl.ds(r + PAD, ROWS)]
                    shift = lax.rem(spot - edge + nz, nz)
                    packed = jnp.where(lane == spot, pltpu.roll(cells, shift, 1), packed)
            edge_send[slot, pl.ds(r, ROWS)] = packed
            return carry

        lax.fori_loop(0, chunks, step, 0)

    def edge_copy(slot):
        return pltpu.make_async_remote_copy(
            src_ref=edge_send.at[slot],
            dst_ref=edge_recv.at[slot],
            send_sem=edge_send_sem.at[slot],
            recv_sem=edge_recv_sem.at[slot],
            device_id={"gz": 1 - gz},
            device_id_type=MESH,
        )

    for load in loads[:4]:
        load.wait()
    pack(first, 6, 0)
    edge_copy(0).start()
    loads[4].wait()
    pack(flow, 3, 1)
    edge_copy(1).start()
    for load in loads[5:]:
        load.wait()
    edge_copy(0).wait_recv()
    edge_copy(1).wait_recv()

    def neighbours(field, f, x, r, packed):
        centre = field[f, x + 1, pl.ds(r + PAD, ROWS)]
        x_plus = field[f, x + 2, pl.ds(r + PAD, ROWS)]
        x_minus = field[f, x, pl.ds(r + PAD, ROWS)]
        y_plus = field[f, x + 1, pl.ds(r + PAD + 1, ROWS)]
        y_minus = field[f, x + 1, pl.ds(r + PAD - 1, ROWS)]
        shift = lax.rem(edge - (f * nx + x) + nz, nz)
        outside = jnp.where(at_edge, pltpu.roll(packed, shift, 1), 0.0)
        z_plus = jnp.where(at_last, outside, pltpu.roll(centre, nz - 1, 1))
        z_minus = jnp.where(at_first, outside, pltpu.roll(centre, 1, 1))
        return centre, x_plus, x_minus, y_plus, y_minus, z_plus, z_minus

    def cell_block(source, slot, is_last, x, k, carry):
        r = pl.multiple_of(k * ROWS, ROWS)
        rows = pl.ds(r, ROWS)
        packed = edge_recv[slot, rows]
        vel = [flow[c, x + 1, pl.ds(r + PAD, ROWS)] for c in range(3)]
        tur = turb[x, rows]
        por = poros[x, rows]
        viscous = VISCOSITY + tur
        if is_last:
            inv_flow = coefs[0, x, rows]
            inv_turb = coefs[1, x, rows]
            coupled = coefs[2, x, rows]
            shear = coefs[3, x, rows]
        else:
            sol = solid[x, rows].astype(jnp.float32)
            inv_wall = 1.0 / wall[x, rows]
            inv_wall2 = inv_wall * inv_wall
            inv_flow = 1.0 / (6.0 * viscous + por + PENALTY * sol)
            inv_turb = 1.0 / (6.0 * viscous + (DESTRUCTION * tur) * inv_wall2)
            coupled = (2.0 * DESTRUCTION * tur) * tur * (inv_wall2 * inv_wall)
            packed_flow = edge_recv[1, rows]
            square = jnp.zeros((ROWS, nz), jnp.float32)
            for c in range(3):
                _, xp, xm, yp, ym, zp, zm = neighbours(flow, c, x, r, packed_flow)
                dx, dy, dz = xp - xm, yp - ym, zp - zm
                square = square + (dx * dx + dy * dy + dz * dz)
            shear = square * (0.25 * COUPLING / 9.0)
            coefs[0, x, rows] = inv_flow
            coefs[1, x, rows] = inv_turb
            coefs[2, x, rows] = coupled
            coefs[3, x, rows] = shear

        near = [neighbours(source, f, x, r, packed) for f in range(6)]
        half = [0.5 * v for v in vel]
        plus = [viscous + h for h in half]
        minus = [viscous - h for h in half]

        def moved(f):
            _, xp, xm, yp, ym, zp, zm = near[f]
            return (
                (plus[0] * xp + minus[0] * xm)
                + (plus[1] * yp + minus[1] * ym)
                + (plus[2] * zp + minus[2] * zm)
            )

        def laplace(f):
            _, xp, xm, yp, ym, zp, zm = near[f]
            return (xp + xm) + (yp + ym) + (zp + zm)

        def rise(f, axis):
            return near[f][1 + 2 * axis] - near[f][2 + 2 * axis]

        old = [n[0] for n in near]
        drive = por + COUPLING * old[4]
        new = [
            (moved(c) + (vel[c] * drive - 0.5 * rise(3, c))) * inv_flow for c in range(3)
        ]
        split = rise(0, 0) + rise(1, 1) + rise(2, 2)
        new.append((laplace(3) - 0.5 * split) * (1.0 / 6.0))
        work = vel[0] * old[0] + vel[1] * old[1] + vel[2] * old[2]
        new.append((moved(4) + (shear + COUPLING * work)) * inv_turb)
        new.append((laplace(5) + coupled * old[4]) * (1.0 / (6.0 + DISTANCE_DAMPING)))
        if is_last:
            for c in range(3):
                new_velocity[c, x, rows] = new[c]
            new_pressure[x, rows] = new[3]
            new_turbulence[x, rows] = new[4]
            new_distance[x, rows] = new[5]
            sol = solid[x, rows].astype(jnp.float32)
            sensitivity[x, rows] = (1.0 - sol) * (
                vel[0] * new[0] + vel[1] * new[1] + vel[2] * new[2]
            )
        else:
            for f in range(6):
                second[f, x + 1, pl.ds(r + PAD, ROWS)] = new[f]
        delta = [(new[f] - old[f]) for f in range(6)]
        square = [d * d for d in delta]
        return (
            carry[0] + (square[0] + square[1] + square[2]),
            carry[1] + square[3],
            carry[2] + square[4],
            carry[3] + square[5],
        )

    def planes(source, slot, is_last, count, place, carry):
        def step(i, carry):
            x = place(lax.div(i, chunks))
            return cell_block(source, slot, is_last, x, lax.rem(i, chunks), carry)

        return lax.fori_loop(0, count * chunks, step, carry, unroll=2)

    def inner(i):
        return i + 1

    def outer(i):
        return i * (nx - 1)

    zero = tuple(jnp.zeros((ROWS, nz), jnp.float32) for _ in range(4))

    totals = planes(first, 0, False, nx - 2, inner, zero)
    wait_faces(faces_of)
    totals = planes(first, 0, False, 2, outer, totals)
    start_faces(later_faces_of)
    for j in range(4):
        sums[pl.ds(j, 1)] = jnp.sum(totals[j], axis=0, keepdims=True)

    pack(second, 6, 2)
    edge_copy(2).start()
    edge_copy(2).wait_recv()
    totals = planes(second, 2, True, nx - 2, inner, zero)
    wait_faces(later_faces_of)
    totals = planes(second, 2, True, 2, outer, totals)
    for j in range(4):
        sums[pl.ds(4 + j, 1)] = jnp.sum(totals[j], axis=0, keepdims=True)

    def sum_copy(k):
        return pltpu.make_async_remote_copy(
            src_ref=sums,
            dst_ref=all_sums.at[k],
            send_sem=sum_send_sem.at[k],
            recv_sem=sum_recv_sem.at[k],
            device_id=others[k],
            device_id_type=MESH,
        )

    for k in range(group - 1):
        sum_copy(k).start()
    finish_faces(faces_of)
    finish_faces(later_faces_of)
    for slot in range(3):
        edge_copy(slot).wait_send()
    whole = sums[...]
    for k in range(group - 1):
        sum_copy(k).wait_recv()
        whole = whole + all_sums[k]
    for k in range(group - 1):
        sum_copy(k).wait_send()
    total = jnp.sum(whole, axis=1, keepdims=True)
    root = jnp.broadcast_to(jnp.sqrt(total + 1e-06), (8, nz))
    norms[...] = root


def local(mesh_shape, *args):
    ngx, ngz = mesh_shape
    assert ngz == 2
    nx, ny, nz = args[1].shape
    assert 6 * nx <= nz and ny % ROWS == 0
    f32 = jnp.float32
    cells = jax.ShapeDtypeStruct((nx, ny, nz), f32)
    group = ngx * ngz
    tall = (nx + 2, ny + 2 * PAD, nz)
    outs = pl.pallas_call(
        functools.partial(kernel, ngx, ngz),
        out_shape=[
            jax.ShapeDtypeStruct((3, nx, ny, nz), f32),
            cells,
            cells,
            cells,
            cells,
            jax.ShapeDtypeStruct((8, nz), f32),
        ],
        in_specs=[pl.BlockSpec(memory_space=pl.ANY)] * 9,
        out_specs=[pl.BlockSpec(memory_space=pltpu.VMEM)] * 6,
        scratch_shapes=[
            pltpu.VMEM((6,) + tall, f32),
            pltpu.VMEM((6,) + tall, f32),
            pltpu.VMEM((3,) + tall, f32),
            pltpu.VMEM((nx, ny, nz), f32),
            pltpu.VMEM((nx, ny, nz), f32),
            pltpu.VMEM((nx, ny, nz), f32),
            pltpu.VMEM((nx, ny, nz), jnp.int32),
            pltpu.VMEM((4, nx, ny, nz), f32),
            pltpu.VMEM((3, ny, nz), f32),
            pltpu.VMEM((3, ny, nz), f32),
            pltpu.VMEM((8, nz), f32),
            pltpu.VMEM((group - 1, 8, nz), f32),
            pltpu.SemaphoreType.DMA((9,)),
            pltpu.SemaphoreType.DMA((2, 6)),
            pltpu.SemaphoreType.DMA((2, 6)),
            pltpu.SemaphoreType.DMA((3,)),
            pltpu.SemaphoreType.DMA((3,)),
            pltpu.SemaphoreType.DMA((group - 1,)),
            pltpu.SemaphoreType.DMA((group - 1,)),
        ],
        compiler_params=pltpu.CompilerParams(
            collective_id=0,
            has_side_effects=True,
            vmem_limit_bytes=52 * 1024 * 1024,
        ),
    )(*args)
    return (*outs[:5], outs[5][:, 0])


def solution(mesh):
    cells = P("gx", "parts", "gz")
    vector = P(None, "gx", "parts", "gz")
    in_specs = (vector, cells, cells, cells, cells, vector, cells, cells, cells)
    out_specs = (vector, cells, cells, cells, cells, P("parts"))
    return jax.shard_map(
        functools.partial(local, (mesh.shape["gx"], mesh.shape["gz"])),
        mesh=mesh,
        in_specs=in_specs,
        out_specs=out_specs,
        check_vma=False,
    )
```

```python
import functools

import jax
import jax.numpy as jnp
from jax import lax
from jax.experimental import pallas as pl
from jax.experimental.pallas import tpu as pltpu
from jax.sharding import PartitionSpec as P

VISCOSITY = 0.5
COUPLING = 0.6
DESTRUCTION = 0.3
DISTANCE_DAMPING = 0.5
PENALTY = 20.0
PAD = 8
ROWS = 16
MESH = pl.DeviceIdType.MESH


def kernel(
    ngx,
    ngz,
    velocity,
    turbulence,
    wall_distance,
    porosity,
    solid_mask,
    adj_velocity,
    adj_pressure,
    adj_turbulence,
    adj_distance,
    new_velocity,
    new_pressure,
    new_turbulence,
    new_distance,
    sensitivity,
    norms,
    first,
    second,
    flow,
    turb,
    wall,
    poros,
    solid,
    coefs,
    edge_send,
    edge_recv,
    sums,
    all_sums,
    held_new_velocity,
    held_new_pressure,
    held_new_turbulence,
    held_new_distance,
    held_sensitivity,
    store_sem,
    load_sem,
    face_send_sem,
    face_recv_sem,
    edge_send_sem,
    edge_recv_sem,
    sum_send_sem,
    sum_recv_sem,
):
    nx, ny, nz = turbulence.shape
    gx = lax.axis_index("gx")
    gz = lax.axis_index("gz")
    me = gx * ngz + gz
    group = ngx * ngz
    has_low = gx > 0
    has_high = gx < ngx - 1
    body = pl.ds(PAD, ny)
    chunks = ny // ROWS

    loads = [
        pltpu.make_async_copy(adj_velocity, first.at[0:3, 1 : nx + 1, body], load_sem.at[0]),
        pltpu.make_async_copy(adj_pressure, first.at[3, 1 : nx + 1, body], load_sem.at[1]),
        pltpu.make_async_copy(adj_turbulence, first.at[4, 1 : nx + 1, body], load_sem.at[2]),
        pltpu.make_async_copy(adj_distance, first.at[5, 1 : nx + 1, body], load_sem.at[3]),
        pltpu.make_async_copy(velocity, flow.at[:, 1 : nx + 1, body], load_sem.at[4]),
        pltpu.make_async_copy(turbulence, turb, load_sem.at[5]),
        pltpu.make_async_copy(wall_distance, wall, load_sem.at[6]),
        pltpu.make_async_copy(porosity, poros, load_sem.at[7]),
        pltpu.make_async_copy(solid_mask, solid, load_sem.at[8]),
    ]
    barrier = pltpu.get_barrier_semaphore()
    others = []
    for k in range(1, group):
        flat = lax.rem(me + k, group)
        others.append({"gx": lax.div(flat, ngz), "gz": lax.rem(flat, ngz)})
    for other in others:
        pl.semaphore_signal(barrier, inc=1, device_id=other, device_id_type=MESH)
    pl.semaphore_wait(barrier, group - 1)

    def face(side, slot, source, target):
        step = -1 if side == 0 else 1
        return pltpu.make_async_remote_copy(
            src_ref=source,
            dst_ref=target,
            send_sem=face_send_sem.at[side, slot],
            recv_sem=face_recv_sem.at[side, slot],
            device_id={"gx": jnp.clip(gx + step, 0, ngx - 1)},
            device_id_type=MESH,
        )

    def faces_of(side):
        plane, halo = (0, nx + 1) if side == 0 else (nx - 1, 0)
        return [
            face(side, 0, adj_velocity.at[:, plane], first.at[0:3, halo, body]),
            face(side, 1, adj_pressure.at[plane], first.at[3, halo, body]),
            face(side, 2, adj_turbulence.at[plane], first.at[4, halo, body]),
            face(side, 3, adj_distance.at[plane], first.at[5, halo, body]),
        ]

    def flow_faces_of(side):
        plane, halo = (0, nx + 1) if side == 0 else (nx - 1, 0)
        return [face(side, 4, velocity.at[:, plane], flow.at[:, halo, body])]

    def later_faces_of(side):
        plane, halo = (1, nx + 1) if side == 0 else (nx, 0)
        return [
            face(side, 5, second.at[0:4, plane, body], second.at[0:4, halo, body]),
            face(side, 6, second.at[5, plane, body], second.at[5, halo, body]),
        ]

    def later_turb_of(side):
        plane, halo = (1, nx + 1) if side == 0 else (nx, 0)
        return [face(side, 7, second.at[4, plane, body], second.at[4, halo, body])]

    sends_to = (has_low, has_high)
    takes_from = (has_high, has_low)

    def start_faces(make):
        for side in (0, 1):
            @pl.when(sends_to[side])
            def _():
                for copy in make(side):
                    copy.start()

    def wait_faces(make):
        for side in (0, 1):
            @pl.when(takes_from[side])
            def _():
                for copy in make(side):
                    copy.wait_recv()

    def finish_faces(make):
        for side in (0, 1):
            @pl.when(sends_to[side])
            def _():
                for copy in make(side):
                    copy.wait_send()

    start_faces(faces_of)
    start_faces(flow_faces_of)
    for load in loads:
        load.start()

    def clear(x, carry):
        blank = jnp.zeros((PAD, nz), jnp.float32)
        for f in range(6):
            for field in (first, second):
                field[f, x, 0:PAD] = blank
                field[f, x, PAD + ny : 2 * PAD + ny] = blank
        for f in range(3):
            flow[f, x, 0:PAD] = blank
            flow[f, x, PAD + ny : 2 * PAD + ny] = blank
        return carry

    lax.fori_loop(1, nx + 1, clear, 0)
    for missing, halo in ((gx == 0, 0), (gx == ngx - 1, nx + 1)):
        @pl.when(missing)
        def _():
            blank = jnp.zeros((ny, nz), jnp.float32)
            for f in range(6):
                first[f, halo, body] = blank
                second[f, halo, body] = blank
            for f in range(3):
                flow[f, halo, body] = blank

    lane = lax.broadcasted_iota(jnp.int32, (ROWS, nz), 1)
    edge = jnp.where(gz == 0, nz - 1, 0)
    at_edge = lane == edge
    at_first = lane == 0
    at_last = lane == nz - 1

    def pack(field, count, slot):
        def step(k, carry):
            r = pl.multiple_of(k * ROWS, ROWS)
            packed = jnp.zeros((ROWS, nz), jnp.float32)
            for f in range(count):
                for x in range(nx):
                    spot = f * nx + x
                    cells = field[f, x + 1, pl.ds(r + PAD, ROWS)]
                    shift = lax.rem(spot - edge + nz, nz)
                    packed = jnp.where(lane == spot, pltpu.roll(cells, shift, 1), packed)
            edge_send[slot, pl.ds(r, ROWS)] = packed
            return carry

        lax.fori_loop(0, chunks, step, 0)

    def edge_copy(slot):
        return pltpu.make_async_remote_copy(
            src_ref=edge_send.at[slot],
            dst_ref=edge_recv.at[slot],
            send_sem=edge_send_sem.at[slot],
            recv_sem=edge_recv_sem.at[slot],
            device_id={"gz": 1 - gz},
            device_id_type=MESH,
        )

    for load in loads[:4]:
        load.wait()
    pack(first, 6, 0)
    edge_copy(0).start()
    loads[4].wait()
    pack(flow, 3, 1)
    edge_copy(1).start()
    for load in loads[5:]:
        load.wait()
    edge_copy(0).wait_recv()
    edge_copy(1).wait_recv()

    def neighbours(field, f, x, r, packed):
        centre = field[f, x + 1, pl.ds(r + PAD, ROWS)]
        x_plus = field[f, x + 2, pl.ds(r + PAD, ROWS)]
        x_minus = field[f, x, pl.ds(r + PAD, ROWS)]
        y_plus = field[f, x + 1, pl.ds(r + PAD + 1, ROWS)]
        y_minus = field[f, x + 1, pl.ds(r + PAD - 1, ROWS)]
        shift = lax.rem(edge - (f * nx + x) + nz, nz)
        outside = jnp.where(at_edge, pltpu.roll(packed, shift, 1), 0.0)
        z_plus = jnp.where(at_last, outside, pltpu.roll(centre, nz - 1, 1))
        z_minus = jnp.where(at_first, outside, pltpu.roll(centre, 1, 1))
        return centre, x_plus, x_minus, y_plus, y_minus, z_plus, z_minus

    def cell_block(source, slot, is_last, groups, x, k, carry):
        r = pl.multiple_of(k * ROWS, ROWS)
        rows = pl.ds(r, ROWS)
        tall_rows = pl.ds(r + PAD, ROWS)
        packed = edge_recv[slot, rows]
        vel = [flow[c, x + 1, tall_rows] for c in range(3)]
        tur = turb[x, rows]
        viscous = VISCOSITY + tur
        half = [0.5 * v for v in vel]
        plus = [viscous + h for h in half]
        minus = [viscous - h for h in half]
        old_turb = source[4, x + 1, tall_rows]
        old = {}
        new = {}

        def near_of(f):
            centre, *sides = neighbours(source, f, x, r, packed)
            old[f] = centre
            return sides

        def moved(sides):
            xp, xm, yp, ym, zp, zm = sides
            return (
                (plus[0] * xp + minus[0] * xm)
                + (plus[1] * yp + minus[1] * ym)
                + (plus[2] * zp + minus[2] * zm)
            )

        def laplace(sides):
            xp, xm, yp, ym, zp, zm = sides
            return (xp + xm) + (yp + ym) + (zp + zm)

        if "rest" in groups:
            por = poros[x, rows]
            if is_last:
                inv_flow = coefs[0, x, rows]
                coupled = coefs[2, x, rows]
            else:
                sol = solid[x, rows].astype(jnp.float32)
                inv_wall = 1.0 / wall[x, rows]
                inv_wall2 = inv_wall * inv_wall
                inv_flow = 1.0 / (6.0 * viscous + por + PENALTY * sol)
                inv_turb = 1.0 / (6.0 * viscous + (DESTRUCTION * tur) * inv_wall2)
                coupled = (2.0 * DESTRUCTION * tur) * tur * (inv_wall2 * inv_wall)
                coefs[0, x, rows] = inv_flow
                coefs[1, x, rows] = inv_turb
                coefs[2, x, rows] = coupled
            drive = por + COUPLING * old_turb
            press = near_of(3)
            split = None
            for c in range(3):
                sides = near_of(c)
                push = 0.5 * (press[2 * c] - press[2 * c + 1])
                new[c] = (moved(sides) + (vel[c] * drive - push)) * inv_flow
                rise = sides[2 * c] - sides[2 * c + 1]
                split = rise if split is None else split + rise
            new[3] = (laplace(press) - 0.5 * split) * (1.0 / 6.0)
            new[5] = (laplace(near_of(5)) + coupled * old_turb) * (
                1.0 / (6.0 + DISTANCE_DAMPING)
            )
        if "turb" in groups:
            if is_last:
                shear = coefs[3, x, rows]
            else:
                packed_flow = edge_recv[1, rows]
                square = jnp.zeros((ROWS, nz), jnp.float32)
                for c in range(3):
                    _, xp, xm, yp, ym, zp, zm = neighbours(flow, c, x, r, packed_flow)
                    dx, dy, dz = xp - xm, yp - ym, zp - zm
                    square = square + (dx * dx + dy * dy + dz * dz)
                shear = square * (0.25 * COUPLING / 9.0)
                coefs[3, x, rows] = shear
            if is_last or "rest" not in groups:
                inv_turb = coefs[1, x, rows]
            u = [source[c, x + 1, tall_rows] for c in range(3)]
            work = vel[0] * u[0] + vel[1] * u[1] + vel[2] * u[2]
            new[4] = (moved(near_of(4)) + (shear + COUPLING * work)) * inv_turb
        if is_last:
            for c in range(3):
                held_new_velocity[c, x, rows] = new[c]
            held_new_pressure[x, rows] = new[3]
            held_new_turbulence[x, rows] = new[4]
            held_new_distance[x, rows] = new[5]
            sol = solid[x, rows].astype(jnp.float32)
            held_sensitivity[x, rows] = (1.0 - sol) * (
                vel[0] * new[0] + vel[1] * new[1] + vel[2] * new[2]
            )
        else:
            for f in new:
                second[f, x + 1, tall_rows] = new[f]
        totals = list(carry)
        for f in new:
            delta = new[f] - old[f]
            j = max(f - 2, 0)
            totals[j] = totals[j] + delta * delta
        return tuple(totals)

    def planes(source, slot, is_last, count, place, carry, groups=("rest", "turb")):
        def step(i, carry):
            x = place(lax.div(i, chunks))
            return cell_block(
                source, slot, is_last, groups, x, lax.rem(i, chunks), carry
            )

        return lax.fori_loop(0, count * chunks, step, carry, unroll=4)

    def inner(i):
        return i + 1

    def outer(i):
        return i * (nx - 1)

    def stores(slot, span):
        pairs = (
            (held_new_pressure, new_pressure),
            (held_new_turbulence, new_turbulence),
            (held_new_distance, new_distance),
            (held_sensitivity, sensitivity),
        )
        copies = [
            pltpu.make_async_copy(
                held_new_velocity.at[:, span], new_velocity.at[:, span], store_sem.at[slot, 4]
            )
        ]
        for i, (held, out) in enumerate(pairs):
            copies.append(
                pltpu.make_async_copy(held.at[span], out.at[span], store_sem.at[slot, i])
            )
        return copies

    all_stores = (
        stores(0, pl.ds(1, nx - 2))
        + stores(1, pl.ds(0, 1))
        + stores(2, pl.ds(nx - 1, 1))
    )

    zero = tuple(jnp.zeros((ROWS, nz), jnp.float32) for _ in range(4))

    totals = planes(first, 0, False, nx - 2, inner, zero)
    wait_faces(faces_of)
    totals = planes(first, 0, False, 2, outer, totals, ("rest",))
    start_faces(later_faces_of)
    wait_faces(flow_faces_of)
    totals = planes(first, 0, False, 2, outer, totals, ("turb",))
    start_faces(later_turb_of)
    for j in range(4):
        sums[pl.ds(j, 1)] = jnp.sum(totals[j], axis=0, keepdims=True)

    pack(second, 6, 2)
    edge_copy(2).start()
    edge_copy(2).wait_recv()
    totals = planes(second, 2, True, nx - 2, inner, zero)
    for store in all_stores[:5]:
        store.start()
    wait_faces(later_faces_of)
    wait_faces(later_turb_of)
    totals = planes(second, 2, True, 2, outer, totals)
    for j in range(4):
        sums[pl.ds(4 + j, 1)] = jnp.sum(totals[j], axis=0, keepdims=True)

    for store in all_stores[5:]:
        store.start()

    def sum_copy(k):
        return pltpu.make_async_remote_copy(
            src_ref=sums,
            dst_ref=all_sums.at[k],
            send_sem=sum_send_sem.at[k],
            recv_sem=sum_recv_sem.at[k],
            device_id=others[k],
            device_id_type=MESH,
        )

    for k in range(group - 1):
        sum_copy(k).start()
    finish_faces(faces_of)
    finish_faces(flow_faces_of)
    finish_faces(later_faces_of)
    finish_faces(later_turb_of)
    for slot in range(3):
        edge_copy(slot).wait_send()
    whole = sums[...]
    for k in range(group - 1):
        sum_copy(k).wait_recv()
        whole = whole + all_sums[k]
    for k in range(group - 1):
        sum_copy(k).wait_send()
    for store in all_stores:
        store.wait()
    total = jnp.sum(whole, axis=1, keepdims=True)
    root = jnp.broadcast_to(jnp.sqrt(total + 1e-06), (8, nz))
    norms[...] = root


def local(mesh_shape, *args):
    ngx, ngz = mesh_shape
    assert ngz == 2
    nx, ny, nz = args[1].shape
    assert 6 * nx <= nz and ny % ROWS == 0
    f32 = jnp.float32
    cells = jax.ShapeDtypeStruct((nx, ny, nz), f32)
    group = ngx * ngz
    tall = (nx + 2, ny + 2 * PAD, nz)
    outs = pl.pallas_call(
        functools.partial(kernel, ngx, ngz),
        out_shape=[
            jax.ShapeDtypeStruct((3, nx, ny, nz), f32),
            cells,
            cells,
            cells,
            cells,
            jax.ShapeDtypeStruct((8, nz), f32),
        ],
        in_specs=[pl.BlockSpec(memory_space=pl.ANY)] * 9,
        out_specs=[pl.BlockSpec(memory_space=pl.ANY)] * 5
        + [pl.BlockSpec(memory_space=pltpu.VMEM)],
        scratch_shapes=[
            pltpu.VMEM((6,) + tall, f32),
            pltpu.VMEM((6,) + tall, f32),
            pltpu.VMEM((3,) + tall, f32),
            pltpu.VMEM((nx, ny, nz), f32),
            pltpu.VMEM((nx, ny, nz), f32),
            pltpu.VMEM((nx, ny, nz), f32),
            pltpu.VMEM((nx, ny, nz), jnp.int32),
            pltpu.VMEM((4, nx, ny, nz), f32),
            pltpu.VMEM((3, ny, nz), f32),
            pltpu.VMEM((3, ny, nz), f32),
            pltpu.VMEM((8, nz), f32),
            pltpu.VMEM((group - 1, 8, nz), f32),
            pltpu.VMEM((3, nx, ny, nz), f32),
            pltpu.VMEM((nx, ny, nz), f32),
            pltpu.VMEM((nx, ny, nz), f32),
            pltpu.VMEM((nx, ny, nz), f32),
            pltpu.VMEM((nx, ny, nz), f32),
            pltpu.SemaphoreType.DMA((3, 5)),
            pltpu.SemaphoreType.DMA((9,)),
            pltpu.SemaphoreType.DMA((2, 8)),
            pltpu.SemaphoreType.DMA((2, 8)),
            pltpu.SemaphoreType.DMA((3,)),
            pltpu.SemaphoreType.DMA((3,)),
            pltpu.SemaphoreType.DMA((group - 1,)),
            pltpu.SemaphoreType.DMA((group - 1,)),
        ],
        compiler_params=pltpu.CompilerParams(
            collective_id=0,
            has_side_effects=True,
            vmem_limit_bytes=52 * 1024 * 1024,
        ),
    )(*args)
    return (*outs[:5], outs[5][:, 0])


def solution(mesh):
    cells = P("gx", "parts", "gz")
    vector = P(None, "gx", "parts", "gz")
    in_specs = (vector, cells, cells, cells, cells, vector, cells, cells, cells)
    out_specs = (vector, cells, cells, cells, cells, P("parts"))
    return jax.shard_map(
        functools.partial(local, (mesh.shape["gx"], mesh.shape["gz"])),
        mesh=mesh,
        in_specs=in_specs,
        out_specs=out_specs,
        check_vma=False,
    )
```

```python
import functools

import jax
import jax.numpy as jnp
from jax import lax
from jax.experimental import pallas as pl
from jax.experimental.pallas import tpu as pltpu
from jax.sharding import PartitionSpec as P

VISCOSITY = 0.5
COUPLING = 0.6
DESTRUCTION = 0.3
DISTANCE_DAMPING = 0.5
PENALTY = 20.0
PAD = 8
ROWS = 16
MESH = pl.DeviceIdType.MESH


def kernel(
    ngx,
    ngz,
    velocity,
    turbulence,
    wall_distance,
    porosity,
    solid_mask,
    adj_velocity,
    adj_pressure,
    adj_turbulence,
    adj_distance,
    new_velocity,
    new_pressure,
    new_turbulence,
    new_distance,
    sensitivity,
    norms,
    first,
    second,
    flow,
    turb,
    wall,
    poros,
    solid,
    coefs,
    edge_send,
    edge_recv,
    sums,
    all_sums,
    held_new_velocity,
    held_new_pressure,
    held_new_turbulence,
    held_new_distance,
    held_sensitivity,
    store_sem,
    load_sem,
    face_send_sem,
    face_recv_sem,
    edge_send_sem,
    edge_recv_sem,
    sum_send_sem,
    sum_recv_sem,
):
    nx, ny, nz = turbulence.shape
    gx = lax.axis_index("gx")
    gz = lax.axis_index("gz")
    me = gx * ngz + gz
    group = ngx * ngz
    has_low = gx > 0
    has_high = gx < ngx - 1
    body = pl.ds(PAD, ny)
    chunks = ny // ROWS

    loads = [
        pltpu.make_async_copy(adj_velocity, first.at[0:3, 1 : nx + 1, body], load_sem.at[0]),
        pltpu.make_async_copy(adj_pressure, first.at[3, 1 : nx + 1, body], load_sem.at[1]),
        pltpu.make_async_copy(adj_turbulence, first.at[4, 1 : nx + 1, body], load_sem.at[2]),
        pltpu.make_async_copy(adj_distance, first.at[5, 1 : nx + 1, body], load_sem.at[3]),
        pltpu.make_async_copy(velocity, flow.at[:, 1 : nx + 1, body], load_sem.at[4]),
        pltpu.make_async_copy(turbulence, turb, load_sem.at[5]),
        pltpu.make_async_copy(wall_distance, wall, load_sem.at[6]),
        pltpu.make_async_copy(porosity, poros, load_sem.at[7]),
        pltpu.make_async_copy(solid_mask, solid, load_sem.at[8]),
    ]
    barrier = pltpu.get_barrier_semaphore()
    others = []
    for k in range(1, group):
        flat = lax.rem(me + k, group)
        others.append({"gx": lax.div(flat, ngz), "gz": lax.rem(flat, ngz)})
    for other in others:
        pl.semaphore_signal(barrier, inc=1, device_id=other, device_id_type=MESH)
    pl.semaphore_wait(barrier, group - 1)

    def face(side, slot, source, target):
        step = -1 if side == 0 else 1
        return pltpu.make_async_remote_copy(
            src_ref=source,
            dst_ref=target,
            send_sem=face_send_sem.at[side, slot],
            recv_sem=face_recv_sem.at[side, slot],
            device_id={"gx": jnp.clip(gx + step, 0, ngx - 1)},
            device_id_type=MESH,
        )

    def faces_of(side):
        plane, halo = (0, nx + 1) if side == 0 else (nx - 1, 0)
        return [
            face(side, 0, adj_velocity.at[:, plane], first.at[0:3, halo, body]),
            face(side, 1, adj_pressure.at[plane], first.at[3, halo, body]),
            face(side, 2, adj_turbulence.at[plane], first.at[4, halo, body]),
            face(side, 3, adj_distance.at[plane], first.at[5, halo, body]),
        ]

    def flow_faces_of(side):
        plane, halo = (0, nx + 1) if side == 0 else (nx - 1, 0)
        return [face(side, 4, velocity.at[:, plane], flow.at[:, halo, body])]

    def later_faces_of(side):
        plane, halo = (1, nx + 1) if side == 0 else (nx, 0)
        return [
            face(side, 5, second.at[0:4, plane, body], second.at[0:4, halo, body]),
            face(side, 6, second.at[5, plane, body], second.at[5, halo, body]),
        ]

    def later_turb_of(side):
        plane, halo = (1, nx + 1) if side == 0 else (nx, 0)
        return [face(side, 7, second.at[4, plane, body], second.at[4, halo, body])]

    sends_to = (has_low, has_high)
    takes_from = (has_high, has_low)

    def start_faces(make):
        for side in (0, 1):
            @pl.when(sends_to[side])
            def _():
                for copy in make(side):
                    copy.start()

    def wait_faces(make):
        for side in (0, 1):
            @pl.when(takes_from[side])
            def _():
                for copy in make(side):
                    copy.wait_recv()

    def finish_faces(make):
        for side in (0, 1):
            @pl.when(sends_to[side])
            def _():
                for copy in make(side):
                    copy.wait_send()

    start_faces(faces_of)
    start_faces(flow_faces_of)
    for load in loads:
        load.start()

    def clear(x, carry):
        blank = jnp.zeros((PAD, nz), jnp.float32)
        for f in range(6):
            for field in (first, second):
                field[f, x, 0:PAD] = blank
                field[f, x, PAD + ny : 2 * PAD + ny] = blank
        for f in range(3):
            flow[f, x, 0:PAD] = blank
            flow[f, x, PAD + ny : 2 * PAD + ny] = blank
        return carry

    lax.fori_loop(1, nx + 1, clear, 0)
    for missing, halo in ((gx == 0, 0), (gx == ngx - 1, nx + 1)):
        @pl.when(missing)
        def _():
            blank = jnp.zeros((ny, nz), jnp.float32)
            for f in range(6):
                first[f, halo, body] = blank
                second[f, halo, body] = blank
            for f in range(3):
                flow[f, halo, body] = blank

    lane = lax.broadcasted_iota(jnp.int32, (ROWS, nz), 1)
    edge = jnp.where(gz == 0, nz - 1, 0)
    at_edge = lane == edge
    at_first = lane == 0
    at_last = lane == nz - 1

    def pack(field, count, slot):
        def step(k, carry):
            r = pl.multiple_of(k * ROWS, ROWS)
            packed = jnp.zeros((ROWS, nz), jnp.float32)
            for f in range(count):
                for x in range(nx):
                    spot = f * nx + x
                    cells = field[f, x + 1, pl.ds(r + PAD, ROWS)]
                    shift = lax.rem(spot - edge + nz, nz)
                    packed = jnp.where(lane == spot, pltpu.roll(cells, shift, 1), packed)
            edge_send[slot, pl.ds(r, ROWS)] = packed
            return carry

        lax.fori_loop(0, chunks, step, 0)

    def edge_copy(slot):
        return pltpu.make_async_remote_copy(
            src_ref=edge_send.at[slot],
            dst_ref=edge_recv.at[slot],
            send_sem=edge_send_sem.at[slot],
            recv_sem=edge_recv_sem.at[slot],
            device_id={"gz": 1 - gz},
            device_id_type=MESH,
        )

    for load in loads[:4]:
        load.wait()
    pack(first, 6, 0)
    edge_copy(0).start()
    loads[4].wait()
    pack(flow, 3, 1)
    edge_copy(1).start()
    for load in loads[5:]:
        load.wait()
    edge_copy(0).wait_recv()
    edge_copy(1).wait_recv()

    def neighbours(field, f, x, r, packed):
        centre = field[f, x + 1, pl.ds(r + PAD, ROWS)]
        x_plus = field[f, x + 2, pl.ds(r + PAD, ROWS)]
        x_minus = field[f, x, pl.ds(r + PAD, ROWS)]
        y_plus = field[f, x + 1, pl.ds(r + PAD + 1, ROWS)]
        y_minus = field[f, x + 1, pl.ds(r + PAD - 1, ROWS)]
        shift = lax.rem(edge - (f * nx + x) + nz, nz)
        outside = jnp.where(at_edge, pltpu.roll(packed, shift, 1), 0.0)
        z_plus = jnp.where(at_last, outside, pltpu.roll(centre, nz - 1, 1))
        z_minus = jnp.where(at_first, outside, pltpu.roll(centre, 1, 1))
        return centre, x_plus, x_minus, y_plus, y_minus, z_plus, z_minus

    def cell_block(source, slot, is_last, groups, x, k, carry):
        r = pl.multiple_of(k * ROWS, ROWS)
        rows = pl.ds(r, ROWS)
        tall_rows = pl.ds(r + PAD, ROWS)
        packed = edge_recv[slot, rows]
        vel = [flow[c, x + 1, tall_rows] for c in range(3)]
        tur = turb[x, rows]
        viscous = VISCOSITY + tur
        half = [0.5 * v for v in vel]
        plus = [viscous + h for h in half]
        minus = [viscous - h for h in half]
        old_turb = source[4, x + 1, tall_rows]
        old = {}
        new = {}

        def near_of(f):
            centre, *sides = neighbours(source, f, x, r, packed)
            old[f] = centre
            return sides

        def moved(sides):
            xp, xm, yp, ym, zp, zm = sides
            return (
                (plus[0] * xp + minus[0] * xm)
                + (plus[1] * yp + minus[1] * ym)
                + (plus[2] * zp + minus[2] * zm)
            )

        def laplace(sides):
            xp, xm, yp, ym, zp, zm = sides
            return (xp + xm) + (yp + ym) + (zp + zm)

        if "rest" in groups:
            por = poros[x, rows]
            if is_last:
                inv_flow = coefs[0, x, rows]
                coupled = coefs[2, x, rows]
            else:
                sol = solid[x, rows].astype(jnp.float32)
                inv_wall = 1.0 / wall[x, rows]
                inv_wall2 = inv_wall * inv_wall
                inv_flow = 1.0 / (6.0 * viscous + por + PENALTY * sol)
                inv_turb = 1.0 / (6.0 * viscous + (DESTRUCTION * tur) * inv_wall2)
                coupled = (2.0 * DESTRUCTION * tur) * tur * (inv_wall2 * inv_wall)
                coefs[0, x, rows] = inv_flow
                coefs[1, x, rows] = inv_turb
                coefs[2, x, rows] = coupled
            drive = por + COUPLING * old_turb
            press = near_of(3)
            split = None
            for c in range(3):
                sides = near_of(c)
                push = 0.5 * (press[2 * c] - press[2 * c + 1])
                new[c] = (moved(sides) + (vel[c] * drive - push)) * inv_flow
                rise = sides[2 * c] - sides[2 * c + 1]
                split = rise if split is None else split + rise
            new[3] = (laplace(press) - 0.5 * split) * (1.0 / 6.0)
            new[5] = (laplace(near_of(5)) + coupled * old_turb) * (
                1.0 / (6.0 + DISTANCE_DAMPING)
            )
        if "turb" in groups:
            if is_last:
                shear = coefs[3, x, rows]
            else:
                packed_flow = edge_recv[1, rows]
                square = jnp.zeros((ROWS, nz), jnp.float32)
                for c in range(3):
                    _, xp, xm, yp, ym, zp, zm = neighbours(flow, c, x, r, packed_flow)
                    dx, dy, dz = xp - xm, yp - ym, zp - zm
                    square = square + (dx * dx + dy * dy + dz * dz)
                shear = square * (0.25 * COUPLING / 9.0)
                coefs[3, x, rows] = shear
            if is_last or "rest" not in groups:
                inv_turb = coefs[1, x, rows]
            u = [source[c, x + 1, tall_rows] for c in range(3)]
            work = vel[0] * u[0] + vel[1] * u[1] + vel[2] * u[2]
            new[4] = (moved(near_of(4)) + (shear + COUPLING * work)) * inv_turb
        if is_last:
            for c in range(3):
                held_new_velocity[c, x, rows] = new[c]
            held_new_pressure[x, rows] = new[3]
            held_new_turbulence[x, rows] = new[4]
            held_new_distance[x, rows] = new[5]
            sol = solid[x, rows].astype(jnp.float32)
            held_sensitivity[x, rows] = (1.0 - sol) * (
                vel[0] * new[0] + vel[1] * new[1] + vel[2] * new[2]
            )
        else:
            for f in new:
                second[f, x + 1, tall_rows] = new[f]
        totals = list(carry)
        for f in new:
            delta = new[f] - old[f]
            j = max(f - 2, 0)
            totals[j] = totals[j] + delta * delta
        return tuple(totals)

    def planes(source, slot, is_last, count, place, carry, groups=("rest", "turb")):
        def step(i, carry):
            x = place(lax.div(i, chunks))
            return cell_block(
                source, slot, is_last, groups, x, lax.rem(i, chunks), carry
            )

        return lax.fori_loop(0, count * chunks, step, carry, unroll=4)

    def inner(i):
        return i + 1

    def outer(i):
        return i * (nx - 1)

    def stores(slot, span):
        pairs = (
            (held_new_pressure, new_pressure),
            (held_new_turbulence, new_turbulence),
            (held_new_distance, new_distance),
            (held_sensitivity, sensitivity),
        )
        copies = [
            pltpu.make_async_copy(
                held_new_velocity.at[:, span], new_velocity.at[:, span], store_sem.at[slot, 4]
            )
        ]
        for i, (held, out) in enumerate(pairs):
            copies.append(
                pltpu.make_async_copy(held.at[span], out.at[span], store_sem.at[slot, i])
            )
        return copies

    all_stores = (
        stores(0, pl.ds(1, nx - 2))
        + stores(1, pl.ds(0, 1))
        + stores(2, pl.ds(nx - 1, 1))
    )

    zero = tuple(jnp.zeros((ROWS, nz), jnp.float32) for _ in range(4))

    totals = planes(first, 0, False, nx - 2, inner, zero)
    wait_faces(faces_of)
    totals = planes(first, 0, False, 2, outer, totals, ("rest",))
    start_faces(later_faces_of)
    wait_faces(flow_faces_of)
    totals = planes(first, 0, False, 2, outer, totals, ("turb",))
    start_faces(later_turb_of)
    for j in range(4):
        sums[pl.ds(j, 1)] = jnp.sum(totals[j], axis=0, keepdims=True)

    pack(second, 6, 2)
    edge_copy(2).start()
    edge_copy(2).wait_recv()
    totals = planes(second, 2, True, nx - 2, inner, zero)
    for store in all_stores[:5]:
        store.start()
    wait_faces(later_faces_of)
    wait_faces(later_turb_of)
    totals = planes(second, 2, True, 2, outer, totals)
    for j in range(4):
        sums[pl.ds(4 + j, 1)] = jnp.sum(totals[j], axis=0, keepdims=True)

    for store in all_stores[5:]:
        store.start()

    def sum_copy(k):
        return pltpu.make_async_remote_copy(
            src_ref=sums,
            dst_ref=all_sums.at[k],
            send_sem=sum_send_sem.at[k],
            recv_sem=sum_recv_sem.at[k],
            device_id=others[k],
            device_id_type=MESH,
        )

    for k in range(group - 1):
        sum_copy(k).start()
    finish_faces(faces_of)
    finish_faces(flow_faces_of)
    finish_faces(later_faces_of)
    finish_faces(later_turb_of)
    for slot in range(3):
        edge_copy(slot).wait_send()
    whole = sums[...]
    for k in range(group - 1):
        sum_copy(k).wait_recv()
        whole = whole + all_sums[k]
    for k in range(group - 1):
        sum_copy(k).wait_send()
    for store in all_stores:
        store.wait()
    total = jnp.sum(whole, axis=1, keepdims=True)
    root = jnp.broadcast_to(jnp.sqrt(total + 1e-06), (8, nz))
    norms[...] = root


def hand_over(*refs):
    for i in range(5):
        refs[5 + i][...] = refs[i][...]


def local(mesh_shape, *args):
    ngx, ngz = mesh_shape
    assert ngz == 2
    nx, ny, nz = args[1].shape
    assert 6 * nx <= nz and ny % ROWS == 0
    f32 = jnp.float32
    cells = jax.ShapeDtypeStruct((nx, ny, nz), f32)
    group = ngx * ngz
    tall = (nx + 2, ny + 2 * PAD, nz)
    outs = pl.pallas_call(
        functools.partial(kernel, ngx, ngz),
        out_shape=[
            jax.ShapeDtypeStruct((3, nx, ny, nz), f32),
            cells,
            cells,
            cells,
            cells,
            jax.ShapeDtypeStruct((8, nz), f32),
        ],
        in_specs=[pl.BlockSpec(memory_space=pl.ANY)] * 9,
        out_specs=[pl.BlockSpec(memory_space=pl.ANY)] * 5
        + [pl.BlockSpec(memory_space=pltpu.VMEM)],
        scratch_shapes=[
            pltpu.VMEM((6,) + tall, f32),
            pltpu.VMEM((6,) + tall, f32),
            pltpu.VMEM((3,) + tall, f32),
            pltpu.VMEM((nx, ny, nz), f32),
            pltpu.VMEM((nx, ny, nz), f32),
            pltpu.VMEM((nx, ny, nz), f32),
            pltpu.VMEM((nx, ny, nz), jnp.int32),
            pltpu.VMEM((4, nx, ny, nz), f32),
            pltpu.VMEM((3, ny, nz), f32),
            pltpu.VMEM((3, ny, nz), f32),
            pltpu.VMEM((8, nz), f32),
            pltpu.VMEM((group - 1, 8, nz), f32),
            pltpu.VMEM((3, nx, ny, nz), f32),
            pltpu.VMEM((nx, ny, nz), f32),
            pltpu.VMEM((nx, ny, nz), f32),
            pltpu.VMEM((nx, ny, nz), f32),
            pltpu.VMEM((nx, ny, nz), f32),
            pltpu.SemaphoreType.DMA((3, 5)),
            pltpu.SemaphoreType.DMA((9,)),
            pltpu.SemaphoreType.DMA((2, 8)),
            pltpu.SemaphoreType.DMA((2, 8)),
            pltpu.SemaphoreType.DMA((3,)),
            pltpu.SemaphoreType.DMA((3,)),
            pltpu.SemaphoreType.DMA((group - 1,)),
            pltpu.SemaphoreType.DMA((group - 1,)),
        ],
        compiler_params=pltpu.CompilerParams(
            collective_id=0,
            has_side_effects=True,
            vmem_limit_bytes=52 * 1024 * 1024,
        ),
    )(*args)
    step = 4
    flat = pl.BlockSpec((step, ny, nz), lambda i: (i, 0, 0))
    tall_block = pl.BlockSpec((3, step, ny, nz), lambda i: (0, i, 0, 0))
    fields = pl.pallas_call(
        hand_over,
        grid=(nx // step,),
        out_shape=[jax.ShapeDtypeStruct(o.shape, o.dtype) for o in outs[:5]],
        in_specs=[tall_block] + [flat] * 4,
        out_specs=[tall_block] + [flat] * 4,
        compiler_params=pltpu.CompilerParams(vmem_limit_bytes=52 * 1024 * 1024),
    )(*outs[:5])
    return (*fields, outs[5][:, 0])


def solution(mesh):
    cells = P("gx", "parts", "gz")
    vector = P(None, "gx", "parts", "gz")
    in_specs = (vector, cells, cells, cells, cells, vector, cells, cells, cells)
    out_specs = (vector, cells, cells, cells, cells, P("parts"))
    return jax.shard_map(
        functools.partial(local, (mesh.shape["gx"], mesh.shape["gz"])),
        mesh=mesh,
        in_specs=in_specs,
        out_specs=out_specs,
        check_vma=False,
    )
```
